32 devices in a mesh: dp: 4 (over z), expert: 2 (over x), head: 4 (over y, core).
Axes of the slice: x: 2, y: 2, z: 4, core: 2. Of those that a mesh axis runs over, the one named last changes fastest.
Arguments:
- hidden_in: bfloat16 [1024, 7168], P(('dp', 'expert'), 'head'), may hold values from -6 to 6
- grad_out: bfloat16 [1024, 7168], P(('dp', 'expert'), 'head'), may hold values from -6 to 6
- expert_ids: int32 [1024, 8], P(('dp', 'expert')), may hold values from 0 to 255, all different within a row; in each aligned block of 128 rows (0 to 127, 128 to 255, ...) at most 8 rows name the same one
- gate_weights: float32 [1024, 8], P(('dp', 'expert')), may hold values from 0.1 to 1
- w_gate: bfloat16 [8, 7168, 2048], P(('dp', 'expert'), None, 'head'), may hold values from -0.0625 to 0.0625
- w_up: bfloat16 [8, 7168, 2048], P(('dp', 'expert'), None, 'head'), may hold values from -0.0625 to 0.0625
- w_down: bfloat16 [8, 2048, 7168], P(('dp', 'expert'), 'head'), may hold values from -0.125 to 0.125
- latent_kv: bfloat16 [1024, 576], P(('dp', 'expert')), may hold values from -16 to 16
- query: bfloat16 [1024, 12288], P('dp', ('expert', 'head')), may hold values from -240 to 240
- d_attn: bfloat16 [1024, 8192], P('dp', ('expert', 'head')), may hold values from -6 to 6
- w_uk: bfloat16 [512, 8192], P(None, ('expert', 'head')), may hold values from -0.25 to 0.25
- w_uv: bfloat16 [512, 8192], P(None, ('expert', 'head')), may hold values from -0.25 to 0.25
- doc_ids: int32 [1024], P('dp'), may hold values from 0 to 15, never falling along the last dimension, each value on 1 to 256 neighbouring positions
Outputs:
- d_hidden: bfloat16 [1024, 7168], P(('dp', 'expert'), 'head')
- d_gates: bfloat16 [1024, 8], P(('dp', 'expert'))
- d_query: bfloat16 [1024, 12288], P('dp', ('expert', 'head'))
- d_latent_kv: bfloat16 [1024, 576], P(('dp', 'expert'), 'head')
The draws below stay inside these ranges and needn't reach their ends.
Inputs may be any that keep to these rules, and one draw needn't show every extreme that they name: `expert_ids`: each row names 8 different experts; in each aligned block of 128 rows (the rows of one device) no expert is named by more than 8 rows, a bound that some block reaches. `doc_ids`: document numbers never fall; each document has 1 to 256 tokens.
All inputs are finite; a program needn't handle non-finite values.
Results may differ from the reference program's by a relative error of at most 0.0089.
Values may be sent and summed in bfloat16 or wider, within the bound.
A program may use at most 128 MiB of HBM per device.

```python
import math
import jax
import jax.numpy as jnp
import numpy as np
from jax import lax

D = 7168
HID = 2048
EXPERTS = 256
TOP = 8
HEADS = 64
LAT = 512
NOPE = 128
ROPE = 64
VD = 128
TOK_DEV = 128
TOKENS = 1024
SEQ = 256
EXP_WIN = 8
CAP = 8
KVW = 576
QK = 192
DOCS = 16
N_DP = 4
N_EXPERT = 2


def latent_base(key):
    normal_part = jnp.clip(jax.random.normal(jax.random.fold_in(key, 11), (TOKENS, KVW), jnp.float32), -4.0, 4.0)
    return normal_part


def draw_latent_kv(key, part):
    return latent_base(key).astype(jnp.bfloat16)


def draw_query(key, part):
    drawn = jnp.clip(jax.random.normal(jax.random.fold_in(key, 31), (TOKENS, HEADS, QK), jnp.float32), -4.0, 4.0)
    return drawn.reshape(TOKENS, HEADS * QK).astype(jnp.bfloat16)


def block_scale(key, extent, pieces, least, top_value):
    level, own = 1.0, jax.random.fold_in(key, 6)
    for position, shards_of in pieces:
        heights = jnp.exp(jax.random.uniform(jax.random.fold_in(own, position), (shards_of,), jnp.float32, least / len(pieces), top_value / len(pieces)))
        level = level * jnp.repeat(heights, extent[position] // shards_of).reshape([-1 if axis == position else 1 for axis in range(len(extent))])
    return level


def split_up(count, total, reach, skew):
    portions = [(1 << 20) // math.isqrt(grade ** skew) + 1 for grade in range(2, count + 1)]
    spare, given = total - reach - (count - 1), [1] * (count - 1)
    while spare > 0:
        free = [i for i in range(count - 1) if given[i] < reach]
        pool, left = sum([portions[i] for i in free]), spare
        for i in free:
            addition = min(reach - given[i], max(1, left * portions[i] // pool), spare)
            given[i] = given[i] + addition
            spare = spare - addition
    return np.array([reach] + given)


def ragged(rng, amount, total, limit, slope):
    if amount == 2:
        one = jax.random.randint(rng, (), max(1, total - limit), min(limit, total - 1) + 1)
        return jnp.stack([one, total - one])
    sizes = jnp.asarray(split_up(amount, total, limit, slope), jnp.int32)
    couples = (amount - 1) // 2
    giver, receiver = sizes[1:1 + 2 * couples:2], sizes[2:2 + 2 * couples:2]
    room = jnp.minimum(giver - 1, limit - receiver)
    shifted = jax.random.randint(jax.random.fold_in(rng, 1), (couples,), 0, 1 << 20) % (room + 1)
    sizes = sizes.at[1:1 + 2 * couples:2].set(giver - shifted).at[2:2 + 2 * couples:2].set(receiver + shifted)
    return sizes[jax.random.permutation(jax.random.fold_in(rng, 2), amount)]


def routed_block(rng, own, number, rows, amount, top, limit, lean):
    sequence = jax.random.permutation(rng, amount)
    heavy_load, usual = shares(amount, rows * top, limit, lean, True), shares(amount, rows * top, limit, lean, False)
    places = jnp.arange(amount)

    def named(lengths, rotation):
        used = int((lengths > 0).sum())
        fixed = max(1, used // 4)
        moved = fixed + (places - fixed + rotation * (used - fixed)) % max(1, amount - fixed)
        return jnp.zeros((amount,), jnp.int32).at[sequence[jnp.where(places < fixed, places, moved)]].set(jnp.asarray(lengths, jnp.int32))

    lengths = jnp.where(number % 4 == 0, named(heavy_load, number // 4), named(usual, number - number // 4 - 1))
    mixed = jax.random.permutation(jax.random.fold_in(own, 3), amount)
    giver, sink = mixed[0:amount // 2 * 2:2], mixed[1:amount // 2 * 2:2]
    room = jnp.minimum(lengths[giver] - 1, limit - lengths[sink]) // 2
    room = jnp.where((giver == sequence[0]) | (sink == sequence[0]) | (lengths[sink] == 0), 0, jnp.maximum(room, 0))
    moved = jax.random.randint(jax.random.fold_in(own, 4), (amount // 2,), 0, 1 << 20) % (room + 1)
    lengths = lengths.at[giver].add(-moved).at[sink].add(moved)
    items = jnp.searchsorted(jnp.cumsum(lengths), jnp.arange(rows * top), side="right").astype(jnp.int32)
    listing = items.reshape(top, rows).T
    listing = listing[jax.random.permutation(jax.random.fold_in(own, 1), rows)]
    rotation = jax.random.randint(jax.random.fold_in(own, 2), (rows, 1), 0, top)
    return jnp.take_along_axis(listing, (jnp.arange(top)[None, :] + rotation) % top, axis=1)


def shares(amount, total, reach, slope, full):
    portions = [(1 << 20) // math.isqrt(grade ** slope) + 1 for grade in range(1, amount + 1)]
    largest = reach if full else min(reach, max(-(-total // amount), total * portions[0] // sum(portions)))
    least = 1 if total - largest >= amount - 1 else 0
    given, rest = [largest] + [least] * (amount - 1), total - largest - least * (amount - 1)
    while rest > 0:
        candidates = [i for i in range(1, amount) if given[i] < largest] or [i for i in range(1, amount) if given[i] < reach]
        pool, left = sum([portions[i] for i in candidates]), rest
        for i in candidates:
            more = min(reach - given[i], max(1, left * portions[i] // pool), rest)
            given[i] = given[i] + more
            rest = rest - more
    return np.array(given)


def noise(rng, shape, scale, most, shards=(), held_as=jnp.bfloat16):
    level = block_scale(rng, shape, shards, -0.22, 0.18) if shards else 1.0
    entries = jax.random.normal(rng, shape, jnp.float32) * scale * level
    return jnp.minimum(jnp.maximum(entries, -most), most).astype(held_as)


def setup_inputs(seed: int = 0) -> dict:
    splits = jax.random.split(jax.random.key(seed), 14)
    hidden_in = noise(splits[0], (TOKENS, D), 1.0, 6.0, ((0, 8), (1, 4)))
    grad_out = noise(splits[1], (TOKENS, D), 1.0, 6.0, ((0, 8), (1, 4)))
    expert_ids_keys = jax.random.split(jax.random.fold_in(splits[2], 1), TOKENS // TOK_DEV)
    expert_ids_turns = jax.random.permutation(jax.random.fold_in(splits[2], 3), TOKENS // TOK_DEV)
    expert_ids = jax.vmap(lambda own, number: routed_block(jax.random.fold_in(splits[2], 2), own, number, TOK_DEV, EXPERTS, TOP, CAP, 2))(expert_ids_keys, expert_ids_turns).reshape((TOKENS, TOP))
    gate_weights = jnp.clip(jnp.exp(math.log(1.0) - 2.3025851 * jax.random.uniform(splits[3], (TOKENS, TOP), jnp.float32) ** block_scale(splits[3], (TOKENS, TOP), ((0, 8),), -0.2, 0.2)), 0.1, 1.0)
    w_gate = noise(splits[4], (EXP_WIN, D, HID), D ** -0.5, 0.0625, ((0, 8), (2, 4)))
    w_up = noise(splits[5], (EXP_WIN, D, HID), D ** -0.5, 0.0625, ((0, 8), (2, 4)))
    w_down = noise(splits[6], (EXP_WIN, HID, D), HID ** -0.5, 0.125, ((0, 8), (1, 4)))
    latent_kv = draw_latent_kv(jax.random.fold_in(splits[13], 71), 0)
    query = draw_query(jax.random.fold_in(splits[13], 71), 0)
    d_attn = noise(splits[9], (TOKENS, HEADS * VD), 1.0, 6.0, ((0, 4), (1, 8)))
    w_uk = noise(splits[10], (LAT, HEADS * NOPE), LAT ** -0.5, 0.25, ((1, 8),))
    w_uv = noise(splits[11], (LAT, HEADS * VD), LAT ** -0.5, 0.25, ((1, 8),))
    doc_ids = jnp.searchsorted(jnp.cumsum(ragged(splits[12], DOCS, TOKENS, SEQ, 1)), jnp.arange(TOKENS), side="right").astype(jnp.int32)
    return dict(hidden_in=hidden_in, grad_out=grad_out, expert_ids=expert_ids, gate_weights=gate_weights, w_gate=w_gate, w_up=w_up, w_down=w_down, latent_kv=latent_kv, query=query, d_attn=d_attn, w_uk=w_uk, w_uv=w_uv, doc_ids=doc_ids)


def expert_part(hidden_in, grad_out, expert_ids, gate_weights, w_gate, w_up, w_down):
    window_size = N_DP * N_EXPERT
    route_ids = expert_ids.reshape(window_size, TOK_DEV * TOP).astype(jnp.int32)
    one_hot = (route_ids[:, :, None] == jnp.arange(window_size, dtype=jnp.int32)[None, None, :]).astype(jnp.int32)
    earlier = jnp.cumsum(one_hot, axis=1) - one_hot
    slot_num = lax.optimization_barrier(jnp.sum(earlier * one_hot, axis=2)).astype(jnp.int32)
    inside = route_ids < window_size
    source = jnp.broadcast_to(jnp.arange(window_size, dtype=jnp.int32)[:, None], route_ids.shape)
    token_num = source * TOK_DEV + (jnp.arange(TOK_DEV * TOP, dtype=jnp.int32) // TOP)[None, :]
    owner = jnp.where(inside, route_ids, window_size).astype(jnp.int32)
    row_index = (source * CAP + slot_num).astype(jnp.int32)
    token_table = jnp.zeros((window_size, window_size * CAP), jnp.int32).at[owner, row_index].set(token_num, mode='drop')
    used_table = jnp.zeros((window_size, window_size * CAP), jnp.int32).at[owner, row_index].set(1, mode='drop')

    def one_expert(expert_in):
        token_rows, used_rows, gate_mat, up_mat, down_mat = expert_in
        rows_x = jnp.where(used_rows[:, None] > 0, jnp.take(hidden_in, token_rows, axis=0), 0)
        rows_dy = jnp.where(used_rows[:, None] > 0, jnp.take(grad_out, token_rows, axis=0), 0)
        gate_pre = jnp.dot(rows_x, gate_mat, preferred_element_type=jnp.float32)
        up_pre = jnp.dot(rows_x, up_mat, preferred_element_type=jnp.float32)
        back_hidden = jnp.dot(rows_dy, down_mat.T, preferred_element_type=jnp.float32)
        sig_val = jax.nn.sigmoid(gate_pre)
        act_val = gate_pre * sig_val
        route_gate = lax.optimization_barrier(jnp.sum(act_val * up_pre * back_hidden, axis=1)).astype(jnp.bfloat16)
        d_up = (back_hidden * act_val).astype(jnp.bfloat16)
        d_pre = (back_hidden * up_pre * sig_val * (1.0 + gate_pre * (1.0 - sig_val))).astype(jnp.bfloat16)
        route_grad = (jnp.dot(d_pre, gate_mat.T, preferred_element_type=jnp.float32) + jnp.dot(d_up, up_mat.T, preferred_element_type=jnp.float32)).astype(jnp.bfloat16)
        return (route_grad, route_gate)
    grad_table, gate_table = lax.map(one_expert, (token_table, used_table, w_gate, w_up, w_down))
    safe_owner = jnp.where(inside, route_ids, 0).reshape(TOKENS, TOP).astype(jnp.int32)
    safe_row = row_index.reshape(TOKENS, TOP)
    inside_tk = inside.reshape(TOKENS, TOP)
    total = jnp.zeros((TOKENS, D), jnp.float32)
    for route_k in range(TOP):
        picked = grad_table[safe_owner[:, route_k], safe_row[:, route_k]].astype(jnp.float32)
        weight_k = jnp.where(inside_tk[:, route_k], gate_weights[:, route_k], 0.0)
        total = total + weight_k[:, None] * picked
    d_hidden = total.astype(jnp.bfloat16)
    d_gates = jnp.where(inside_tk, gate_table[safe_owner, safe_row], 0).astype(jnp.bfloat16)
    return (d_hidden, d_gates)

def attention_part(latent_kv, query, d_attn, w_uk, w_uv, doc_ids):
    score_scale = 1.0 / math.sqrt(NOPE + ROPE)
    kv_seq = latent_kv.reshape(N_DP, SEQ, KVW)
    query_seq = query.reshape(N_DP, SEQ, HEADS, QK).transpose(0, 2, 1, 3)
    dout_seq = d_attn.reshape(N_DP, SEQ, HEADS, VD).transpose(0, 2, 1, 3)
    doc_seq = doc_ids.reshape(N_DP, SEQ)
    key_mats = w_uk.reshape(LAT, HEADS, NOPE).transpose(1, 0, 2)
    value_mats = w_uv.reshape(LAT, HEADS, VD).transpose(1, 0, 2)
    positions = jnp.arange(SEQ, dtype=jnp.int32)

    def one_sequence(seq_in):
        kv_rows, query_heads, dout_heads, doc_row = seq_in
        latent = kv_rows[:, :LAT]
        rope_key = kv_rows[:, LAT:]
        allowed = (positions[None, :] <= positions[:, None]) & (doc_row[None, :] == doc_row[:, None])

        def one_head(head_in):
            query_h, dout_h, key_mat, value_mat = head_in
            key_nope = jnp.dot(latent, key_mat, preferred_element_type=jnp.float32).astype(jnp.bfloat16)
            values = jnp.dot(latent, value_mat, preferred_element_type=jnp.float32).astype(jnp.bfloat16)
            keys = jnp.concatenate([key_nope, rope_key], axis=1)
            scores = jnp.dot(query_h, keys.T, preferred_element_type=jnp.float32) * score_scale
            scores = jnp.where(allowed, scores, -1e+30)
            top_score = lax.optimization_barrier(jnp.max(scores, axis=1, keepdims=True))
            expd = jnp.exp(scores - top_score)
            probs = expd / lax.optimization_barrier(jnp.sum(expd, axis=1, keepdims=True))
            dprobs = jnp.dot(dout_h, values.T, preferred_element_type=jnp.float32)
            inner = lax.optimization_barrier(jnp.sum(probs * dprobs, axis=1, keepdims=True))
            dscore = (probs * (dprobs - inner) * score_scale).astype(jnp.bfloat16)
            prob_low = probs.astype(jnp.bfloat16)
            d_q = jnp.dot(dscore, keys, preferred_element_type=jnp.float32).astype(jnp.bfloat16)
            d_key = jnp.dot(dscore.T, query_h, preferred_element_type=jnp.float32).astype(jnp.bfloat16)
            d_val = jnp.dot(prob_low.T, dout_h, preferred_element_type=jnp.float32).astype(jnp.bfloat16)
            lat_grad = jnp.dot(d_key[:, :NOPE], key_mat.T, preferred_element_type=jnp.float32) + jnp.dot(d_val, value_mat.T, preferred_element_type=jnp.float32)
            return (d_q, lat_grad, d_key[:, NOPE:].astype(jnp.float32))
        d_q, lat_grads, rope_grads = lax.map(one_head, (query_heads, dout_heads, key_mats, value_mats))
        d_lat = jnp.concatenate([lax.optimization_barrier(jnp.sum(lat_grads, axis=0)), lax.optimization_barrier(jnp.sum(rope_grads, axis=0))], axis=1)
        return (d_q, d_lat.astype(jnp.bfloat16))
    d_q, d_lat = lax.map(one_sequence, (kv_seq, query_seq, dout_seq, doc_seq))
    d_query = d_q.transpose(0, 2, 1, 3).reshape(TOKENS, HEADS * QK)
    return (d_query, d_lat.reshape(TOKENS, KVW))

def reference(hidden_in, grad_out, expert_ids, gate_weights, w_gate, w_up, w_down, latent_kv, query, d_attn, w_uk, w_uv, doc_ids):
    d_hidden, d_gates = expert_part(hidden_in, grad_out, expert_ids, gate_weights, w_gate, w_up, w_down)
    d_query, d_latent_kv = attention_part(latent_kv, query, d_attn, w_uk, w_uv, doc_ids)
    return (d_hidden, d_gates, d_query, d_latent_kv)
```

```python
import math

import jax
import jax.numpy as jnp
from jax import lax
from jax.sharding import PartitionSpec as P

TOP = 8
LAT = 512
NOPE = 128
ROPE = 64
VD = 128
CAP = 8


CONTRACT_LAST = (((1,), (1,)), ((), ()))


def expert_backward(rows_x, rows_dy, gate_mat, up_mat, down_mat):
    gate_pre = jnp.dot(rows_x, gate_mat, preferred_element_type=jnp.float32)
    up_pre = jnp.dot(rows_x, up_mat, preferred_element_type=jnp.float32)
    back_hidden = lax.dot_general(
        rows_dy, down_mat, CONTRACT_LAST, preferred_element_type=jnp.float32
    )
    sig_val = jax.nn.sigmoid(gate_pre)
    act_val = gate_pre * sig_val
    gate_part = jnp.sum(act_val * up_pre * back_hidden, axis=1)
    d_up = (back_hidden * act_val).astype(jnp.bfloat16)
    d_pre = (back_hidden * up_pre * sig_val * (1.0 + gate_pre * (1.0 - sig_val))).astype(
        jnp.bfloat16
    )
    row_part = lax.dot_general(
        d_pre, gate_mat, CONTRACT_LAST, preferred_element_type=jnp.float32
    ) + lax.dot_general(d_up, up_mat, CONTRACT_LAST, preferred_element_type=jnp.float32)
    return (row_part, gate_part)


def routing(expert_ids, gate_weights, window_size):
    tok_local = expert_ids.shape[0]
    names = expert_ids[:, :, None] == jnp.arange(window_size, dtype=jnp.int32)[None, None, :]
    member = jnp.any(names, axis=1)
    weight = jnp.sum(jnp.where(names, gate_weights[:, :, None], 0.0), axis=1)
    before = jnp.tril(jnp.ones((tok_local, tok_local), jnp.bfloat16), -1)
    earlier = jnp.dot(before, member.astype(jnp.bfloat16), preferred_element_type=jnp.float32)
    slot_num = jnp.where(member, earlier.astype(jnp.int32), -1)
    hits = slot_num[:, :, None] == jnp.arange(CAP, dtype=jnp.int32)[None, None, :]
    slots = window_size * CAP
    combine = jnp.where(hits, weight[:, :, None], 0.0).reshape(tok_local, slots)
    hits = hits.reshape(tok_local, slots)
    return (hits, combine, names)


def expert_half(hidden_in, grad_out, expert_ids, gate_weights, w_gate, w_up, w_down):
    window_size = lax.axis_size("dp") * lax.axis_size("expert")
    head_count = lax.axis_size("head")
    tok_local, width = hidden_in.shape
    slots = window_size * CAP
    hits, combine, names = routing(expert_ids, gate_weights, window_size)
    pick = hits.astype(jnp.bfloat16)
    rows = jnp.concatenate([hidden_in, grad_out], axis=1)
    send = lax.dot_general(
        pick, rows, (((0,), (0,)), ((), ())), preferred_element_type=jnp.float32
    ).astype(jnp.bfloat16)
    send = send.reshape(window_size, CAP, 2 * width)
    got = lax.all_to_all(send, ("dp", "expert"), split_axis=0, concat_axis=0, tiled=True)
    got = lax.all_gather(got.reshape(slots, 2 * width), "head", axis=0, tiled=False)
    flat_x = got[:, :, :width].transpose(1, 0, 2).reshape(slots, head_count * width)
    flat_dy = got[:, :, width:].transpose(1, 0, 2).reshape(slots, head_count * width)
    row_part, gate_part = expert_backward(flat_x, flat_dy, w_gate[0], w_up[0], w_down[0])
    parts = row_part.astype(jnp.bfloat16).reshape(slots, head_count, width)
    gate_cols = jnp.broadcast_to(
        gate_part.astype(jnp.bfloat16)[:, None, None], (slots, head_count, 128)
    )
    parts = jnp.concatenate([parts, gate_cols], axis=2).transpose(1, 0, 2)
    parts = lax.all_to_all(parts, "head", split_axis=0, concat_axis=0, tiled=True)
    summed = jnp.sum(parts.astype(jnp.float32), axis=0).astype(jnp.bfloat16)
    summed = summed.reshape(window_size, CAP, width + 128)
    back = lax.all_to_all(summed, ("dp", "expert"), split_axis=0, concat_axis=0, tiled=True)
    back = back.reshape(slots, width + 128)
    high = combine.astype(jnp.bfloat16)
    rest = combine - high.astype(jnp.float32)
    low = rest.astype(jnp.bfloat16)
    flat_back = back[:, :width]
    d_hidden = jnp.dot(
        jnp.concatenate([high, low], axis=1),
        jnp.concatenate([flat_back, flat_back], axis=0),
        preferred_element_type=jnp.float32,
    ).astype(jnp.bfloat16)
    gate_of = jnp.where(hits, back[:, width].astype(jnp.float32)[None, :], 0.0)
    gate_of = jnp.sum(gate_of.reshape(tok_local, window_size, CAP), axis=2)
    d_gates = jnp.sum(jnp.where(names, gate_of[:, None, :], 0.0), axis=2).astype(jnp.bfloat16)
    return (d_hidden, d_gates)


def attention_half(latent_kv, query, d_attn, w_uk, w_uv, doc_ids):
    seq_len = query.shape[0]
    heads_here = w_uk.shape[1] // NOPE
    score_scale = 1.0 / math.sqrt(NOPE + ROPE)
    w_both = jnp.concatenate([w_uk, w_uv], axis=1)
    piece = lax.all_gather(latent_kv, "expert", axis=0, tiled=True)
    lifted = jnp.dot(piece[:, :LAT], w_both, preferred_element_type=jnp.float32).astype(
        jnp.bfloat16
    )
    keyvals = jnp.concatenate([lifted, piece[:, LAT:]], axis=1)
    key_nope = keyvals[:, : heads_here * NOPE].reshape(seq_len, heads_here, NOPE)
    all_values = keyvals[:, heads_here * NOPE : heads_here * (NOPE + VD)].reshape(
        seq_len, heads_here, VD
    )
    rope_key = keyvals[:, heads_here * (NOPE + VD) :]
    all_keys = jnp.concatenate(
        [key_nope, jnp.broadcast_to(rope_key[:, None, :], (seq_len, heads_here, ROPE))], axis=2
    )
    queries = query.reshape(seq_len, heads_here, NOPE + ROPE)
    douts = d_attn.reshape(seq_len, heads_here, VD)
    positions = jnp.arange(seq_len, dtype=jnp.int32)
    block_rows = min(512, seq_len)
    dkey_sum = jnp.zeros((seq_len, heads_here, NOPE + ROPE), jnp.float32)
    dval_sum = jnp.zeros((seq_len, heads_here, VD), jnp.float32)
    dq_blocks = []
    for block_num in range(seq_len // block_rows):
        first_row = block_num * block_rows
        query_blk = queries[first_row : first_row + block_rows]
        dout_blk = douts[first_row : first_row + block_rows]
        scores = (
            jnp.einsum("qhd,khd->hqk", query_blk, all_keys, preferred_element_type=jnp.float32)
            * score_scale
        )
        allowed = (positions[None, :] <= positions[first_row : first_row + block_rows, None]) & (
            doc_ids[None, :] == doc_ids[first_row : first_row + block_rows, None]
        )
        scores = jnp.where(allowed[None], scores, -1e30)
        top_score = jnp.max(scores, axis=2, keepdims=True)
        expd = jnp.exp(scores - top_score)
        probs = expd / jnp.sum(expd, axis=2, keepdims=True)
        dprobs = jnp.einsum(
            "qhd,khd->hqk", dout_blk, all_values, preferred_element_type=jnp.float32
        )
        inner = jnp.sum(probs * dprobs, axis=2, keepdims=True)
        dscore = (probs * (dprobs - inner) * score_scale).astype(jnp.bfloat16)
        prob_low = probs.astype(jnp.bfloat16)
        dq_blocks.append(
            jnp.einsum("hqk,khd->qhd", dscore, all_keys, preferred_element_type=jnp.float32).astype(
                jnp.bfloat16
            )
        )
        dkey_sum = dkey_sum + jnp.einsum(
            "hqk,qhd->khd", dscore, query_blk, preferred_element_type=jnp.float32
        )
        dval_sum = dval_sum + jnp.einsum(
            "hqk,qhd->khd", prob_low, dout_blk, preferred_element_type=jnp.float32
        )
    d_query = jnp.concatenate(dq_blocks, axis=0).reshape(seq_len, heads_here * (NOPE + ROPE))
    dkey_low = dkey_sum.astype(jnp.bfloat16)
    dval_low = dval_sum.astype(jnp.bfloat16)
    row_count = lax.axis_size("expert") * latent_kv.shape[0]
    nope_flat = dkey_low[:, :, :NOPE].reshape(row_count, heads_here * NOPE)
    lat_term = lax.dot_general(
        nope_flat, w_uk, CONTRACT_LAST, preferred_element_type=jnp.float32
    ) + lax.dot_general(
        dval_low.reshape(row_count, heads_here * VD),
        w_uv,
        CONTRACT_LAST,
        preferred_element_type=jnp.float32,
    )
    rope_term = jnp.sum(dkey_low[:, :, NOPE:].astype(jnp.float32), axis=1)
    own_rows = lax.psum_scatter(
        jnp.concatenate([lat_term, rope_term], axis=1), "expert", scatter_dimension=0, tiled=True
    )
    d_latent = lax.psum_scatter(own_rows, "head", scatter_dimension=1, tiled=True)
    return (d_query, d_latent.astype(jnp.bfloat16))


def body(
    hidden_in,
    grad_out,
    expert_ids,
    gate_weights,
    w_gate,
    w_up,
    w_down,
    latent_kv,
    query,
    d_attn,
    w_uk,
    w_uv,
    doc_ids,
):
    d_query, d_latent_kv = attention_half(latent_kv, query, d_attn, w_uk, w_uv, doc_ids)
    d_hidden, d_gates = expert_half(
        hidden_in, grad_out, expert_ids, gate_weights, w_gate, w_up, w_down
    )
    return (d_hidden, d_gates, d_query, d_latent_kv)


def solution(mesh):
    placed = (
        P(("dp", "expert"), "head"),
        P(("dp", "expert"), "head"),
        P(("dp", "expert"), None),
        P(("dp", "expert"), None),
        P(("dp", "expert"), None, "head"),
        P(("dp", "expert"), None, "head"),
        P(("dp", "expert"), "head", None),
        P(("dp", "expert"), None),
        P("dp", ("expert", "head")),
        P("dp", ("expert", "head")),
        P(None, ("expert", "head")),
        P(None, ("expert", "head")),
        P("dp"),
    )
    return jax.shard_map(
        body,
        mesh=mesh,
        in_specs=placed,
        out_specs=(
            P(("dp", "expert"), "head"),
            P(("dp", "expert"), None),
            P("dp", ("expert", "head")),
            P(("dp", "expert"), "head"),
        ),
        check_vma=False,
    )
```

```python
import functools
import math

import jax
import jax.numpy as jnp
from jax import lax
from jax.experimental import pallas as pl
from jax.experimental.pallas import tpu as pltpu
from jax.sharding import PartitionSpec as P

TOP = 8
LAT = 512
NOPE = 128
ROPE = 64
VD = 128
CAP = 8


CONTRACT_LAST = (((1,), (1,)), ((), ()))


MESH = pl.DeviceIdType.MESH
LANES = 128


def greet(peers):
    barrier = pltpu.get_barrier_semaphore()
    for peer in peers:
        pl.semaphore_signal(barrier, inc=1, device_id=peer, device_id_type=MESH)


def met(peers):
    pl.semaphore_wait(pltpu.get_barrier_semaphore(), len(peers))


def window_peers(experts, window):
    me = lax.axis_index("dp") * experts + lax.axis_index("expert")
    spots = [lax.rem(me + d, window) for d in range(1, window)]
    head = lax.axis_index("head")
    return me, spots, [(spot // experts, lax.rem(spot, experts), head) for spot in spots]


def dispatch_kernel(
    experts, window, send_ref, lat_ref, got_ref, piece_ref, out_sem, in_sem, lat_out, lat_in, own
):
    me, spots, peers = window_peers(experts, window)
    dp, expert, head = (lax.axis_index(name) for name in ("dp", "expert", "head"))
    greet(peers)
    own_rows = pltpu.make_async_copy(send_ref.at[me], got_ref.at[me], own.at[0])
    own_lat = pltpu.make_async_copy(lat_ref, piece_ref.at[expert], own.at[1])
    own_rows.start()
    own_lat.start()
    met(peers)
    copies = []
    for d in range(1, experts):
        copies.append(
            pltpu.make_async_remote_copy(
                src_ref=lat_ref,
                dst_ref=piece_ref.at[expert],
                send_sem=lat_out.at[d - 1],
                recv_sem=lat_in.at[d - 1],
                device_id=(dp, lax.rem(expert + d, experts), head),
                device_id_type=MESH,
            )
        )
    for num, (spot, peer) in enumerate(zip(spots, peers)):
        copies.append(
            pltpu.make_async_remote_copy(
                src_ref=send_ref.at[spot],
                dst_ref=got_ref.at[me],
                send_sem=out_sem.at[num],
                recv_sem=in_sem.at[num],
                device_id=peer,
                device_id_type=MESH,
            )
        )
    for copy in copies:
        copy.start()
    own_rows.wait()
    own_lat.wait()
    for copy in copies:
        copy.wait()


def dispatch(send, latent):
    experts = lax.axis_size("expert")
    window = lax.axis_size("dp") * experts
    hbm = pl.BlockSpec(memory_space=pl.ANY)
    return pl.pallas_call(
        functools.partial(dispatch_kernel, experts, window),
        out_shape=(
            jax.ShapeDtypeStruct(send.shape, send.dtype),
            jax.ShapeDtypeStruct((experts,) + latent.shape, latent.dtype),
        ),
        in_specs=[hbm, hbm],
        out_specs=(hbm, hbm),
        scratch_shapes=[
            pltpu.SemaphoreType.DMA((window - 1,)),
            pltpu.SemaphoreType.DMA((window - 1,)),
            pltpu.SemaphoreType.DMA((experts - 1,)),
            pltpu.SemaphoreType.DMA((experts - 1,)),
            pltpu.SemaphoreType.DMA((2,)),
        ],
        compiler_params=pltpu.CompilerParams(collective_id=1, has_side_effects=True),
        name="dispatch",
    )(send, latent)


def expert_kernel(
    experts,
    window,
    heads,
    got_ref,
    wg_ref,
    wu_ref,
    wd_ref,
    back_ref,
    rows_buf,
    wg_buf,
    wu_buf,
    wd_buf,
    part_buf,
    land_buf,
    sum_buf,
    back_buf,
    load_sem,
    part_out,
    part_in,
    back_out,
    back_in,
):
    me, spots, peers = window_peers(experts, window)
    dp, expert, head = (lax.axis_index(name) for name in ("dp", "expert", "head"))
    width = got_ref.shape[3]
    slots = window * CAP
    half = width // 2
    order = list(range(heads))
    spot_of = [lax.rem(head + d, heads) for d in order]
    head_peers = [(dp, expert, spot_of[d]) for d in order]
    everyone = head_peers[1:] + peers
    loads = []
    for d in order:
        cols = pl.ds(pl.multiple_of(spot_of[d] * width, LANES), width)
        loads.append(
            [
                pltpu.make_async_copy(got_ref.at[spot_of[d]], rows_buf.at[d], load_sem.at[0, d]),
                pltpu.make_async_copy(wg_ref.at[0, cols, :], wg_buf.at[d], load_sem.at[1, d]),
                pltpu.make_async_copy(wu_ref.at[0, cols, :], wu_buf.at[d], load_sem.at[2, d]),
                pltpu.make_async_copy(wd_ref.at[0, :, cols], wd_buf.at[d], load_sem.at[3, d]),
            ]
        )
        for copy in loads[d]:
            copy.start()
    greet(everyone)
    gate_pre = up_pre = back_hidden = None
    for d in order:
        loads[d][0].wait()
        rows = rows_buf[d].astype(jnp.float32)
        rows_x = rows[:, :CAP].reshape(slots, width).astype(jnp.bfloat16)
        rows_dy = rows[:, CAP:].reshape(slots, width).astype(jnp.bfloat16)
        loads[d][1].wait()
        term = jnp.dot(rows_x, wg_buf[d], preferred_element_type=jnp.float32)
        gate_pre = term if d == 0 else gate_pre + term
        loads[d][2].wait()
        term = jnp.dot(rows_x, wu_buf[d], preferred_element_type=jnp.float32)
        up_pre = term if d == 0 else up_pre + term
        loads[d][3].wait()
        term = lax.dot_general(
            rows_dy, wd_buf[d], CONTRACT_LAST, preferred_element_type=jnp.float32
        )
        back_hidden = term if d == 0 else back_hidden + term
    sig_val = jax.nn.sigmoid(gate_pre)
    act_val = gate_pre * sig_val
    gate_part = jnp.sum(act_val * up_pre * back_hidden, axis=1, keepdims=True)
    d_up = (back_hidden * act_val).astype(jnp.bfloat16)
    d_pre = (back_hidden * up_pre * sig_val * (1.0 + gate_pre * (1.0 - sig_val))).astype(
        jnp.bfloat16
    )
    gate_high = gate_part.astype(jnp.bfloat16).astype(jnp.float32)
    lane = lax.broadcasted_iota(jnp.int32, (slots, LANES), 1)
    gate_cols = jnp.where(lane < LANES // 2, gate_high, gate_part - gate_high)
    met(everyone)
    copies = []
    for d in order[1:] + [0]:
        part = lax.dot_general(
            d_pre, wg_buf[d], CONTRACT_LAST, preferred_element_type=jnp.float32
        ) + lax.dot_general(d_up, wu_buf[d], CONTRACT_LAST, preferred_element_type=jnp.float32)
        if d == 0:
            total, gate_total = part, gate_cols
            continue
        part_buf[d - 1, :, :width] = part.astype(jnp.bfloat16)
        part_buf[d - 1, :, width:] = gate_cols.astype(jnp.bfloat16)
        copies.append(
            pltpu.make_async_remote_copy(
                src_ref=part_buf.at[d - 1],
                dst_ref=land_buf.at[d - 1],
                send_sem=part_out.at[d - 1],
                recv_sem=part_in.at[d - 1],
                device_id=head_peers[d],
                device_id_type=MESH,
            )
        )
        copies[-1].start()
    for d in order[1:]:
        copies[d - 1].wait()
        total = total + land_buf[d - 1, :, :width].astype(jnp.float32)
        gate_total = gate_total + land_buf[d - 1, :, width:].astype(jnp.float32)
    gate_sum = gate_total[:, :1] + gate_total[:, LANES // 2 : LANES // 2 + 1]
    gate_cols = jnp.broadcast_to(gate_sum, (slots, LANES)).reshape(window, CAP, LANES)
    total = total.reshape(window, CAP, width)
    packed = jnp.concatenate(
        [
            jnp.concatenate([total[:, :, :half], gate_cols], axis=2),
            jnp.concatenate([total[:, :, half:], gate_cols], axis=2),
        ],
        axis=1,
    ).astype(jnp.bfloat16)
    sum_buf[...] = packed
    copies = []
    for num, (spot, peer) in enumerate(zip(spots, peers)):
        copies.append(
            pltpu.make_async_remote_copy(
                src_ref=sum_buf.at[spot],
                dst_ref=back_buf.at[me],
                send_sem=back_out.at[num],
                recv_sem=back_in.at[num],
                device_id=peer,
                device_id_type=MESH,
            )
        )
        copies[-1].start()
    own = pltpu.make_async_copy(sum_buf.at[me], back_buf.at[me], load_sem.at[0, 0])
    own.start()
    own.wait()
    for copy in copies:
        copy.wait()
    back_ref[...] = back_buf[...]


def expert_backward(got, w_gate, w_up, w_down):
    experts = lax.axis_size("expert")
    window = lax.axis_size("dp") * experts
    heads, _, tile, width = got.shape
    hidden = w_gate.shape[2]
    slots = window * CAP
    hbm = pl.BlockSpec(memory_space=pl.ANY)
    back = (window, tile, width // 2 + LANES)
    dma = pltpu.SemaphoreType.DMA
    return pl.pallas_call(
        functools.partial(expert_kernel, experts, window, heads),
        out_shape=jax.ShapeDtypeStruct(back, jnp.bfloat16),
        in_specs=[hbm] * 4,
        out_specs=pl.BlockSpec(memory_space=pltpu.VMEM),
        scratch_shapes=[
            pltpu.VMEM((heads, window, tile, width), jnp.bfloat16),
            pltpu.VMEM((heads, width, hidden), jnp.bfloat16),
            pltpu.VMEM((heads, width, hidden), jnp.bfloat16),
            pltpu.VMEM((heads, hidden, width), jnp.bfloat16),
            pltpu.VMEM((heads - 1, slots, width + LANES), jnp.bfloat16),
            pltpu.VMEM((heads - 1, slots, width + LANES), jnp.bfloat16),
            pltpu.VMEM(back, jnp.bfloat16),
            pltpu.VMEM(back, jnp.bfloat16),
            dma((4, heads)),
            dma((heads - 1,)),
            dma((heads - 1,)),
            dma((window - 1,)),
            dma((window - 1,)),
        ],
        compiler_params=pltpu.CompilerParams(
            collective_id=2, has_side_effects=True, vmem_limit_bytes=56 * 1024 * 1024
        ),
        cost_estimate=pl.CostEstimate(
            flops=10 * slots * hidden * width * heads,
            bytes_accessed=6 * hidden * width * heads,
            transcendentals=slots * hidden,
        ),
        name="experts",
    )(got, w_gate, w_up, w_down)


def routing(expert_ids, gate_weights, window_size):
    tok_local = expert_ids.shape[0]
    names = expert_ids[:, :, None] == jnp.arange(window_size, dtype=jnp.int32)[None, None, :]
    member = jnp.any(names, axis=1)
    weight = jnp.sum(jnp.where(names, gate_weights[:, :, None], 0.0), axis=1)
    before = jnp.tril(jnp.ones((tok_local, tok_local), jnp.bfloat16), -1)
    earlier = jnp.dot(before, member.astype(jnp.bfloat16), preferred_element_type=jnp.float32)
    slot_num = jnp.where(member, earlier.astype(jnp.int32), -1)
    hits = slot_num[:, :, None] == jnp.arange(CAP, dtype=jnp.int32)[None, None, :]
    slots = window_size * CAP
    combine = jnp.where(hits, weight[:, :, None], 0.0).reshape(tok_local, slots)
    hits = hits.reshape(tok_local, slots)
    return (hits, combine, names)


def expert_send(hidden_in, grad_out, hits):
    tok_local, width = hidden_in.shape
    window_size = hits.shape[1] // CAP
    pick = hits.astype(jnp.bfloat16)
    rows = jnp.concatenate([hidden_in, grad_out], axis=1)
    send = lax.dot_general(
        pick, rows, (((0,), (0,)), ((), ())), preferred_element_type=jnp.float32
    ).astype(jnp.bfloat16)
    send = send.reshape(window_size, CAP, 2 * width)
    return jnp.concatenate([send[:, :, :width], send[:, :, width:]], axis=1)


def expert_half(got, hits, combine, names, w_gate, w_up, w_down):
    tok_local, _, window_size = names.shape
    slots = window_size * CAP
    got = lax.all_gather(got, "head", axis=0, tiled=False)
    back = expert_backward(got, w_gate, w_up, w_down)
    half = back.shape[2] - LANES
    flat_back = jnp.concatenate([back[:, :CAP, :half], back[:, CAP:, :half]], axis=2)
    flat_back = flat_back.reshape(slots, 2 * half)
    flat_gate = back[:, :CAP, half].reshape(slots)
    high = combine.astype(jnp.bfloat16)
    rest = combine - high.astype(jnp.float32)
    low = rest.astype(jnp.bfloat16)
    d_hidden = jnp.dot(
        jnp.concatenate([high, low], axis=1),
        jnp.concatenate([flat_back, flat_back], axis=0),
        preferred_element_type=jnp.float32,
    ).astype(jnp.bfloat16)
    gate_of = jnp.where(hits, flat_gate.astype(jnp.float32)[None, :], 0.0)
    gate_of = jnp.sum(gate_of.reshape(tok_local, window_size, CAP), axis=2)
    d_gates = jnp.sum(jnp.where(names, gate_of[:, None, :], 0.0), axis=2).astype(jnp.bfloat16)
    return (d_hidden, d_gates)


def attention_half(latent_kv, piece, query, d_attn, w_uk, w_uv, doc_ids):
    seq_len = query.shape[0]
    heads_here = w_uk.shape[1] // NOPE
    score_scale = 1.0 / math.sqrt(NOPE + ROPE)
    w_both = jnp.concatenate([w_uk, w_uv], axis=1)
    piece = piece.reshape(seq_len, piece.shape[2])
    lifted = jnp.dot(piece[:, :LAT], w_both, preferred_element_type=jnp.float32).astype(
        jnp.bfloat16
    )
    keyvals = jnp.concatenate([lifted, piece[:, LAT:]], axis=1)
    key_nope = keyvals[:, : heads_here * NOPE].reshape(seq_len, heads_here, NOPE)
    all_values = keyvals[:, heads_here * NOPE : heads_here * (NOPE + VD)].reshape(
        seq_len, heads_here, VD
    )
    rope_key = keyvals[:, heads_here * (NOPE + VD) :]
    all_keys = jnp.concatenate(
        [key_nope, jnp.broadcast_to(rope_key[:, None, :], (seq_len, heads_here, ROPE))], axis=2
    )
    queries = query.reshape(seq_len, heads_here, NOPE + ROPE)
    douts = d_attn.reshape(seq_len, heads_here, VD)
    positions = jnp.arange(seq_len, dtype=jnp.int32)
    block_rows = min(512, seq_len)
    dkey_sum = jnp.zeros((seq_len, heads_here, NOPE + ROPE), jnp.float32)
    dval_sum = jnp.zeros((seq_len, heads_here, VD), jnp.float32)
    dq_blocks = []
    for block_num in range(seq_len // block_rows):
        first_row = block_num * block_rows
        query_blk = queries[first_row : first_row + block_rows]
        dout_blk = douts[first_row : first_row + block_rows]
        scores = (
            jnp.einsum("qhd,khd->hqk", query_blk, all_keys, preferred_element_type=jnp.float32)
            * score_scale
        )
        allowed = (positions[None, :] <= positions[first_row : first_row + block_rows, None]) & (
            doc_ids[None, :] == doc_ids[first_row : first_row + block_rows, None]
        )
        scores = jnp.where(allowed[None], scores, -1e30)
        top_score = jnp.max(scores, axis=2, keepdims=True)
        expd = jnp.exp(scores - top_score)
        probs = expd / jnp.sum(expd, axis=2, keepdims=True)
        dprobs = jnp.einsum(
            "qhd,khd->hqk", dout_blk, all_values, preferred_element_type=jnp.float32
        )
        inner = jnp.sum(probs * dprobs, axis=2, keepdims=True)
        dscore = (probs * (dprobs - inner) * score_scale).astype(jnp.bfloat16)
        prob_low = probs.astype(jnp.bfloat16)
        dq_blocks.append(
            jnp.einsum("hqk,khd->qhd", dscore, all_keys, preferred_element_type=jnp.float32).astype(
                jnp.bfloat16
            )
        )
        dkey_sum = dkey_sum + jnp.einsum(
            "hqk,qhd->khd", dscore, query_blk, preferred_element_type=jnp.float32
        )
        dval_sum = dval_sum + jnp.einsum(
            "hqk,qhd->khd", prob_low, dout_blk, preferred_element_type=jnp.float32
        )
    d_query = jnp.concatenate(dq_blocks, axis=0).reshape(seq_len, heads_here * (NOPE + ROPE))
    dkey_low = dkey_sum.astype(jnp.bfloat16)
    dval_low = dval_sum.astype(jnp.bfloat16)
    row_count = lax.axis_size("expert") * latent_kv.shape[0]
    nope_flat = dkey_low[:, :, :NOPE].reshape(row_count, heads_here * NOPE)
    lat_term = lax.dot_general(
        nope_flat, w_uk, CONTRACT_LAST, preferred_element_type=jnp.float32
    ) + lax.dot_general(
        dval_low.reshape(row_count, heads_here * VD),
        w_uv,
        CONTRACT_LAST,
        preferred_element_type=jnp.float32,
    )
    rope_term = jnp.sum(dkey_low[:, :, NOPE:].astype(jnp.float32), axis=1)
    own_rows = lax.psum_scatter(
        jnp.concatenate([lat_term, rope_term], axis=1), "expert", scatter_dimension=0, tiled=True
    )
    d_latent = lax.psum_scatter(own_rows, "head", scatter_dimension=1, tiled=True)
    return (d_query, d_latent.astype(jnp.bfloat16))


def body(
    hidden_in,
    grad_out,
    expert_ids,
    gate_weights,
    w_gate,
    w_up,
    w_down,
    latent_kv,
    query,
    d_attn,
    w_uk,
    w_uv,
    doc_ids,
):
    window_size = lax.axis_size("dp") * lax.axis_size("expert")
    hits, combine, names = routing(expert_ids, gate_weights, window_size)
    send = expert_send(hidden_in, grad_out, hits)
    got, piece = dispatch(send, latent_kv)
    d_query, d_latent_kv = attention_half(latent_kv, piece, query, d_attn, w_uk, w_uv, doc_ids)
    d_hidden, d_gates = expert_half(got, hits, combine, names, w_gate, w_up, w_down)
    return (d_hidden, d_gates, d_query, d_latent_kv)


def solution(mesh):
    placed = (
        P(("dp", "expert"), "head"),
        P(("dp", "expert"), "head"),
        P(("dp", "expert"), None),
        P(("dp", "expert"), None),
        P(("dp", "expert"), None, "head"),
        P(("dp", "expert"), None, "head"),
        P(("dp", "expert"), "head", None),
        P(("dp", "expert"), None),
        P("dp", ("expert", "head")),
        P("dp", ("expert", "head")),
        P(None, ("expert", "head")),
        P(None, ("expert", "head")),
        P("dp"),
    )
    return jax.shard_map(
        body,
        mesh=mesh,
        in_specs=placed,
        out_specs=(
            P(("dp", "expert"), "head"),
            P(("dp", "expert"), None),
            P("dp", ("expert", "head")),
            P(("dp", "expert"), "head"),
        ),
        check_vma=False,
    )
```

```python
import functools
import math

import jax
import jax.numpy as jnp
from jax import lax
from jax.experimental import pallas as pl
from jax.experimental.pallas import tpu as pltpu
from jax.sharding import PartitionSpec as P

TOP = 8
LAT = 512
NOPE = 128
ROPE = 64
VD = 128
CAP = 8


CONTRACT_LAST = (((1,), (1,)), ((), ()))


MESH = pl.DeviceIdType.MESH
LANES = 128


def greet(peers):
    barrier = pltpu.get_barrier_semaphore()
    for peer in peers:
        pl.semaphore_signal(barrier, inc=1, device_id=peer, device_id_type=MESH)


def met(peers):
    pl.semaphore_wait(pltpu.get_barrier_semaphore(), len(peers))


def window_peers(experts, window):
    me = lax.axis_index("dp") * experts + lax.axis_index("expert")
    spots = [lax.rem(me + d, window) for d in range(1, window)]
    head = lax.axis_index("head")
    return me, spots, [(spot // experts, lax.rem(spot, experts), head) for spot in spots]


def dispatch_kernel(
    experts, window, send_ref, lat_ref, got_ref, piece_ref, out_sem, in_sem, lat_out, lat_in, own
):
    me, spots, peers = window_peers(experts, window)
    dp, expert, head = (lax.axis_index(name) for name in ("dp", "expert", "head"))
    greet(peers)
    own_rows = pltpu.make_async_copy(send_ref.at[me], got_ref.at[me], own.at[0])
    own_lat = pltpu.make_async_copy(lat_ref, piece_ref.at[expert], own.at[1])
    own_rows.start()
    own_lat.start()
    met(peers)
    copies = []
    for d in range(1, experts):
        copies.append(
            pltpu.make_async_remote_copy(
                src_ref=lat_ref,
                dst_ref=piece_ref.at[expert],
                send_sem=lat_out.at[d - 1],
                recv_sem=lat_in.at[d - 1],
                device_id=(dp, lax.rem(expert + d, experts), head),
                device_id_type=MESH,
            )
        )
    for num, (spot, peer) in enumerate(zip(spots, peers)):
        copies.append(
            pltpu.make_async_remote_copy(
                src_ref=send_ref.at[spot],
                dst_ref=got_ref.at[me],
                send_sem=out_sem.at[num],
                recv_sem=in_sem.at[num],
                device_id=peer,
                device_id_type=MESH,
            )
        )
    for copy in copies:
        copy.start()
    own_rows.wait()
    own_lat.wait()
    for copy in copies:
        copy.wait()


def dispatch(send, latent):
    experts = lax.axis_size("expert")
    window = lax.axis_size("dp") * experts
    hbm = pl.BlockSpec(memory_space=pl.ANY)
    return pl.pallas_call(
        functools.partial(dispatch_kernel, experts, window),
        out_shape=(
            jax.ShapeDtypeStruct(send.shape, send.dtype),
            jax.ShapeDtypeStruct((experts,) + latent.shape, latent.dtype),
        ),
        in_specs=[hbm, hbm],
        out_specs=(hbm, hbm),
        scratch_shapes=[
            pltpu.SemaphoreType.DMA((window - 1,)),
            pltpu.SemaphoreType.DMA((window - 1,)),
            pltpu.SemaphoreType.DMA((experts - 1,)),
            pltpu.SemaphoreType.DMA((experts - 1,)),
            pltpu.SemaphoreType.DMA((2,)),
        ],
        compiler_params=pltpu.CompilerParams(collective_id=1, has_side_effects=True),
        name="dispatch",
    )(send, latent)


def expert_kernel(
    experts,
    window,
    heads,
    got_ref,
    wg_ref,
    wu_ref,
    wd_ref,
    back_ref,
    rows_buf,
    wg_buf,
    wu_buf,
    wd_buf,
    part_buf,
    land_buf,
    sum_buf,
    back_buf,
    load_sem,
    part_out,
    part_in,
    back_out,
    back_in,
):
    me, spots, peers = window_peers(experts, window)
    dp, expert, head = (lax.axis_index(name) for name in ("dp", "expert", "head"))
    width = got_ref.shape[3]
    slots = window * CAP
    half = width // 2
    order = list(range(heads))
    spot_of = [lax.rem(head + d, heads) for d in order]
    head_peers = [(dp, expert, spot_of[d]) for d in order]
    everyone = head_peers[1:] + peers
    loads = []
    for d in order:
        cols = pl.ds(pl.multiple_of(spot_of[d] * width, LANES), width)
        loads.append(
            [
                pltpu.make_async_copy(got_ref.at[spot_of[d]], rows_buf.at[d], load_sem.at[0, d]),
                pltpu.make_async_copy(wg_ref.at[0, cols, :], wg_buf.at[d], load_sem.at[1, d]),
                pltpu.make_async_copy(wu_ref.at[0, cols, :], wu_buf.at[d], load_sem.at[2, d]),
                pltpu.make_async_copy(wd_ref.at[0, :, cols], wd_buf.at[d], load_sem.at[3, d]),
            ]
        )
        for copy in loads[d]:
            copy.start()
    greet(everyone)
    gate_pre = up_pre = back_hidden = None
    for d in order:
        loads[d][0].wait()
        rows = rows_buf[d].astype(jnp.float32)
        rows_x = rows[:, :CAP].reshape(slots, width).astype(jnp.bfloat16)
        rows_dy = rows[:, CAP:].reshape(slots, width).astype(jnp.bfloat16)
        loads[d][1].wait()
        term = jnp.dot(rows_x, wg_buf[d], preferred_element_type=jnp.float32)
        gate_pre = term if d == 0 else gate_pre + term
        loads[d][2].wait()
        term = jnp.dot(rows_x, wu_buf[d], preferred_element_type=jnp.float32)
        up_pre = term if d == 0 else up_pre + term
        loads[d][3].wait()
        term = lax.dot_general(
            rows_dy, wd_buf[d], CONTRACT_LAST, preferred_element_type=jnp.float32
        )
        back_hidden = term if d == 0 else back_hidden + term
    sig_val = jax.nn.sigmoid(gate_pre)
    act_val = gate_pre * sig_val
    gate_part = jnp.sum(act_val * up_pre * back_hidden, axis=1, keepdims=True)
    d_up = (back_hidden * act_val).astype(jnp.bfloat16)
    d_pre = (back_hidden * up_pre * sig_val * (1.0 + gate_pre * (1.0 - sig_val))).astype(
        jnp.bfloat16
    )
    gate_high = gate_part.astype(jnp.bfloat16).astype(jnp.float32)
    lane = lax.broadcasted_iota(jnp.int32, (slots, LANES), 1)
    gate_cols = jnp.where(lane < LANES // 2, gate_high, gate_part - gate_high)
    met(everyone)
    copies = []
    for d in order[1:] + [0]:
        part = lax.dot_general(
            d_pre, wg_buf[d], CONTRACT_LAST, preferred_element_type=jnp.float32
        ) + lax.dot_general(d_up, wu_buf[d], CONTRACT_LAST, preferred_element_type=jnp.float32)
        if d == 0:
            total, gate_total = part, gate_cols
            continue
        part_buf[d - 1, :, :width] = part.astype(jnp.bfloat16)
        part_buf[d - 1, :, width:] = gate_cols.astype(jnp.bfloat16)
        copies.append(
            pltpu.make_async_remote_copy(
                src_ref=part_buf.at[d - 1],
                dst_ref=land_buf.at[d - 1],
                send_sem=part_out.at[d - 1],
                recv_sem=part_in.at[d - 1],
                device_id=head_peers[d],
                device_id_type=MESH,
            )
        )
        copies[-1].start()
    for d in order[1:]:
        copies[d - 1].wait()
        total = total + land_buf[d - 1, :, :width].astype(jnp.float32)
        gate_total = gate_total + land_buf[d - 1, :, width:].astype(jnp.float32)
    gate_sum = gate_total[:, :1] + gate_total[:, LANES // 2 : LANES // 2 + 1]
    gate_cols = jnp.broadcast_to(gate_sum, (slots, LANES)).reshape(window, CAP, LANES)
    total = total.reshape(window, CAP, width)
    packed = jnp.concatenate(
        [
            jnp.concatenate([total[:, :, :half], gate_cols], axis=2),
            jnp.concatenate([total[:, :, half:], gate_cols], axis=2),
        ],
        axis=1,
    ).astype(jnp.bfloat16)
    sum_buf[...] = packed
    copies = []
    for num, (spot, peer) in enumerate(zip(spots, peers)):
        copies.append(
            pltpu.make_async_remote_copy(
                src_ref=sum_buf.at[spot],
                dst_ref=back_buf.at[me],
                send_sem=back_out.at[num],
                recv_sem=back_in.at[num],
                device_id=peer,
                device_id_type=MESH,
            )
        )
        copies[-1].start()
    own = pltpu.make_async_copy(sum_buf.at[me], back_buf.at[me], load_sem.at[0, 0])
    own.start()
    own.wait()
    for copy in copies:
        copy.wait()
    back_ref[...] = back_buf[...]


def expert_backward(got, w_gate, w_up, w_down):
    experts = lax.axis_size("expert")
    window = lax.axis_size("dp") * experts
    heads, _, tile, width = got.shape
    hidden = w_gate.shape[2]
    slots = window * CAP
    hbm = pl.BlockSpec(memory_space=pl.ANY)
    back = (window, tile, width // 2 + LANES)
    dma = pltpu.SemaphoreType.DMA
    return pl.pallas_call(
        functools.partial(expert_kernel, experts, window, heads),
        out_shape=jax.ShapeDtypeStruct(back, jnp.bfloat16),
        in_specs=[hbm] * 4,
        out_specs=pl.BlockSpec(memory_space=pltpu.VMEM),
        scratch_shapes=[
            pltpu.VMEM((heads, window, tile, width), jnp.bfloat16),
            pltpu.VMEM((heads, width, hidden), jnp.bfloat16),
            pltpu.VMEM((heads, width, hidden), jnp.bfloat16),
            pltpu.VMEM((heads, hidden, width), jnp.bfloat16),
            pltpu.VMEM((heads - 1, slots, width + LANES), jnp.bfloat16),
            pltpu.VMEM((heads - 1, slots, width + LANES), jnp.bfloat16),
            pltpu.VMEM(back, jnp.bfloat16),
            pltpu.VMEM(back, jnp.bfloat16),
            dma((4, heads)),
            dma((heads - 1,)),
            dma((heads - 1,)),
            dma((window - 1,)),
            dma((window - 1,)),
        ],
        compiler_params=pltpu.CompilerParams(
            collective_id=2, has_side_effects=True, vmem_limit_bytes=56 * 1024 * 1024
        ),
        cost_estimate=pl.CostEstimate(
            flops=10 * slots * hidden * width * heads,
            bytes_accessed=6 * hidden * width * heads,
            transcendentals=slots * hidden,
        ),
        name="experts",
    )(got, w_gate, w_up, w_down)


def routing(expert_ids, gate_weights, window_size):
    tok_local = expert_ids.shape[0]
    names = expert_ids[:, :, None] == jnp.arange(window_size, dtype=jnp.int32)[None, None, :]
    member = jnp.any(names, axis=1)
    weight = jnp.sum(jnp.where(names, gate_weights[:, :, None], 0.0), axis=1)
    before = jnp.tril(jnp.ones((tok_local, tok_local), jnp.bfloat16), -1)
    earlier = jnp.dot(before, member.astype(jnp.bfloat16), preferred_element_type=jnp.float32)
    slot_num = jnp.where(member, earlier.astype(jnp.int32), -1)
    hits = slot_num[:, :, None] == jnp.arange(CAP, dtype=jnp.int32)[None, None, :]
    slots = window_size * CAP
    combine = jnp.where(hits, weight[:, :, None], 0.0).reshape(tok_local, slots)
    hits = hits.reshape(tok_local, slots)
    return (hits, combine, names)


def expert_send(hidden_in, grad_out, hits):
    tok_local, width = hidden_in.shape
    window_size = hits.shape[1] // CAP
    pick = hits.astype(jnp.bfloat16)
    rows = jnp.concatenate([hidden_in, grad_out], axis=1)
    send = lax.dot_general(
        pick, rows, (((0,), (0,)), ((), ())), preferred_element_type=jnp.float32
    ).astype(jnp.bfloat16)
    send = send.reshape(window_size, CAP, 2 * width)
    return jnp.concatenate([send[:, :, :width], send[:, :, width:]], axis=1)


def expert_half(back, hits, combine, names):
    tok_local, _, window_size = names.shape
    slots = window_size * CAP
    half = back.shape[2] - LANES
    flat_back = jnp.concatenate([back[:, :CAP, :half], back[:, CAP:, :half]], axis=2)
    flat_back = flat_back.reshape(slots, 2 * half)
    flat_gate = back[:, :CAP, half].reshape(slots)
    high = combine.astype(jnp.bfloat16)
    rest = combine - high.astype(jnp.float32)
    low = rest.astype(jnp.bfloat16)
    d_hidden = jnp.dot(
        jnp.concatenate([high, low], axis=1),
        jnp.concatenate([flat_back, flat_back], axis=0),
        preferred_element_type=jnp.float32,
    ).astype(jnp.bfloat16)
    gate_of = jnp.where(hits, flat_gate.astype(jnp.float32)[None, :], 0.0)
    gate_of = jnp.sum(gate_of.reshape(tok_local, window_size, CAP), axis=2)
    d_gates = jnp.sum(jnp.where(names, gate_of[:, None, :], 0.0), axis=2).astype(jnp.bfloat16)
    return (d_hidden, d_gates)


def attention_half(latent_kv, piece, query, d_attn, w_uk, w_uv, doc_ids):
    seq_len = query.shape[0]
    heads_here = w_uk.shape[1] // NOPE
    score_scale = 1.0 / math.sqrt(NOPE + ROPE)
    w_both = jnp.concatenate([w_uk, w_uv], axis=1)
    piece = piece.reshape(seq_len, piece.shape[2])
    lifted = jnp.dot(piece[:, :LAT], w_both, preferred_element_type=jnp.float32).astype(
        jnp.bfloat16
    )
    keyvals = jnp.concatenate([lifted, piece[:, LAT:]], axis=1)
    key_nope = keyvals[:, : heads_here * NOPE].reshape(seq_len, heads_here, NOPE)
    all_values = keyvals[:, heads_here * NOPE : heads_here * (NOPE + VD)].reshape(
        seq_len, heads_here, VD
    )
    rope_key = keyvals[:, heads_here * (NOPE + VD) :]
    all_keys = jnp.concatenate(
        [key_nope, jnp.broadcast_to(rope_key[:, None, :], (seq_len, heads_here, ROPE))], axis=2
    )
    queries = query.reshape(seq_len, heads_here, NOPE + ROPE)
    douts = d_attn.reshape(seq_len, heads_here, VD)
    positions = jnp.arange(seq_len, dtype=jnp.int32)
    block_rows = min(512, seq_len)
    dkey_sum = jnp.zeros((seq_len, heads_here, NOPE + ROPE), jnp.float32)
    dval_sum = jnp.zeros((seq_len, heads_here, VD), jnp.float32)
    dq_blocks = []
    for block_num in range(seq_len // block_rows):
        first_row = block_num * block_rows
        query_blk = queries[first_row : first_row + block_rows]
        dout_blk = douts[first_row : first_row + block_rows]
        scores = (
            jnp.einsum("qhd,khd->hqk", query_blk, all_keys, preferred_element_type=jnp.float32)
            * score_scale
        )
        allowed = (positions[None, :] <= positions[first_row : first_row + block_rows, None]) & (
            doc_ids[None, :] == doc_ids[first_row : first_row + block_rows, None]
        )
        scores = jnp.where(allowed[None], scores, -1e30)
        top_score = jnp.max(scores, axis=2, keepdims=True)
        expd = jnp.exp(scores - top_score)
        probs = expd / jnp.sum(expd, axis=2, keepdims=True)
        dprobs = jnp.einsum(
            "qhd,khd->hqk", dout_blk, all_values, preferred_element_type=jnp.float32
        )
        inner = jnp.sum(probs * dprobs, axis=2, keepdims=True)
        dscore = (probs * (dprobs - inner) * score_scale).astype(jnp.bfloat16)
        prob_low = probs.astype(jnp.bfloat16)
        dq_blocks.append(
            jnp.einsum("hqk,khd->qhd", dscore, all_keys, preferred_element_type=jnp.float32).astype(
                jnp.bfloat16
            )
        )
        dkey_sum = dkey_sum + jnp.einsum(
            "hqk,qhd->khd", dscore, query_blk, preferred_element_type=jnp.float32
        )
        dval_sum = dval_sum + jnp.einsum(
            "hqk,qhd->khd", prob_low, dout_blk, preferred_element_type=jnp.float32
        )
    d_query = jnp.concatenate(dq_blocks, axis=0).reshape(seq_len, heads_here * (NOPE + ROPE))
    dkey_low = dkey_sum.astype(jnp.bfloat16)
    dval_low = dval_sum.astype(jnp.bfloat16)
    row_count = lax.axis_size("expert") * latent_kv.shape[0]
    nope_flat = dkey_low[:, :, :NOPE].reshape(row_count, heads_here * NOPE)
    lat_term = lax.dot_general(
        nope_flat, w_uk, CONTRACT_LAST, preferred_element_type=jnp.float32
    ) + lax.dot_general(
        dval_low.reshape(row_count, heads_here * VD),
        w_uv,
        CONTRACT_LAST,
        preferred_element_type=jnp.float32,
    )
    rope_term = jnp.sum(dkey_low[:, :, NOPE:].astype(jnp.float32), axis=1)
    cols = latent_kv.shape[1] // lax.axis_size("head")
    terms = jnp.concatenate([lat_term, rope_term], axis=1)
    terms = terms.reshape(lax.axis_size("expert"), latent_kv.shape[0], lax.axis_size("head"), cols)
    return (d_query, terms.transpose(0, 2, 1, 3).reshape(-1, cols))


def body(
    hidden_in,
    grad_out,
    expert_ids,
    gate_weights,
    w_gate,
    w_up,
    w_down,
    latent_kv,
    query,
    d_attn,
    w_uk,
    w_uv,
    doc_ids,
):
    window_size = lax.axis_size("dp") * lax.axis_size("expert")
    hits, combine, names = routing(expert_ids, gate_weights, window_size)
    send = expert_send(hidden_in, grad_out, hits)
    got, piece = dispatch(send, latent_kv)
    got = lax.all_gather(got, "head", axis=0, tiled=False)
    d_query, terms = attention_half(latent_kv, piece, query, d_attn, w_uk, w_uv, doc_ids)
    got, terms, d_query = lax.optimization_barrier((got, terms, d_query))
    d_latent_kv = lax.psum_scatter(
        terms, ("expert", "head"), scatter_dimension=0, tiled=True
    ).astype(jnp.bfloat16)
    back = expert_backward(got, w_gate, w_up, w_down)
    back, d_latent_kv = lax.optimization_barrier((back, d_latent_kv))
    d_hidden, d_gates = expert_half(back, hits, combine, names)
    return (d_hidden, d_gates, d_query, d_latent_kv)


def solution(mesh):
    placed = (
        P(("dp", "expert"), "head"),
        P(("dp", "expert"), "head"),
        P(("dp", "expert"), None),
        P(("dp", "expert"), None),
        P(("dp", "expert"), None, "head"),
        P(("dp", "expert"), None, "head"),
        P(("dp", "expert"), "head", None),
        P(("dp", "expert"), None),
        P("dp", ("expert", "head")),
        P("dp", ("expert", "head")),
        P(None, ("expert", "head")),
        P(None, ("expert", "head")),
        P("dp"),
    )
    return jax.shard_map(
        body,
        mesh=mesh,
        in_specs=placed,
        out_specs=(
            P(("dp", "expert"), "head"),
            P(("dp", "expert"), None),
            P("dp", ("expert", "head")),
            P(("dp", "expert"), "head"),
        ),
        check_vma=False,
    )
```
